32 devices in a mesh: dp: 8 (over z, x), seq: 4 (over y, core).
Axes of the slice: x: 2, y: 2, z: 4, core: 2. Of those that a mesh axis runs over, the one named last changes fastest.
Arguments:
- tokens: bfloat16 [8, 2048, 768], P('dp', 'seq'), may hold values from -6 to 6
- lengths: int32 [8], P('dp'), may hold values from 512 to 2048, as said below
- cotangent: bfloat16 [8, 2048, 768], P('dp', 'seq'), may hold values from -6 to 6
- w_query: bfloat16 [768, 768], replicated, may hold values from -0.21875 to 0.21875
- w_key: bfloat16 [768, 768], replicated, may hold values from -0.21875 to 0.21875
- w_value: bfloat16 [768, 768], replicated, may hold values from -0.21875 to 0.21875
- w_out: bfloat16 [768, 768], replicated, may hold values from -0.875 to 0.875
- w_up: bfloat16 [768, 3072], replicated, may hold values from -0.21875 to 0.21875
- w_down: bfloat16 [3072, 768], replicated, may hold values from -0.109375 to 0.109375
- shared_a: bfloat16 [768, 1024], replicated, may hold values from -0.21875 to 0.21875
- shared_b: bfloat16 [1024, 768], replicated, may hold values from -0.1875 to 0.1875
- vec_biases: float32 [6, 768], replicated, may hold values from -3 to 3
- bias_up: float32 [3072], replicated, may hold values from -3 to 3
- norm_gains: float32 [2, 768], replicated, may hold values from 0.25 to 1.75
- scale_d: float32 [2, 1024], replicated, may hold values from -3 to 3
- scale_b: float32 [2, 768], replicated, may hold values from -3 to 3
- mom_d: float32 [2, 1024], replicated, may hold values from -384 to 384
- sec_d: float32 [2, 1024], replicated, may hold values from 2048 to 32768
- mom_b: float32 [2, 768], replicated, may hold values from -384 to 384
- sec_b: float32 [2, 768], replicated, may hold values from 2048 to 32768
Outputs:
- activations: bfloat16 [8, 2048, 768], P('dp', 'seq')
- grad_input: float32 [8, 2048, 768], P('dp', 'seq')
- moment_d: float32 [2, 1024], replicated
- second_d: float32 [2, 1024], replicated
- moment_b: float32 [2, 768], replicated
- second_b: float32 [2, 768], replicated
- new_d: float32 [2, 1024], replicated
- new_b: float32 [2, 768], replicated
- copy_d: bfloat16 [2, 1024], replicated
- copy_b: bfloat16 [2, 768], replicated
The draws below stay inside these ranges and needn't reach their ends.
Inputs may be any that keep to these rules, and one draw needn't show every extreme that they name: `lengths`: of the 1 sequence of one index of dp, one holds all 2048 positions; the others hold 512 or more.
All inputs are finite; a program needn't handle non-finite values.
Results may differ from the reference program's by a relative error of at most 0.018.
Values may be sent and summed in bfloat16 or wider, within the bound.
No kernel may reach another device: no remote copies, remote signals or barrier semaphores. Data moves between devices by JAX's collectives and lax.ppermute only.
A program may use at most 192 MiB of HBM per device.

```python
import math
import jax
import jax.numpy as jnp
from jax import lax

D = 768
HEADS = 12
HEAD = 64
FF = 3072
RANK = 1024
STEP = 10
SEQS = 1
SPAN = 2048
BATCH = 8


def draw_lengths(key, part):
    key = jax.random.fold_in(key, 7)
    key_base, key_pick = jax.random.split(key)
    base = jax.random.randint(key_base, (BATCH,), SPAN // 4, SPAN + 1)
    pick = jax.random.randint(key_pick, (BATCH // SEQS,), 0, SEQS)
    slot = jnp.arange(BATCH, dtype=jnp.int32) % SEQS
    full = slot == jnp.repeat(pick, SEQS)
    return jnp.where(full, SPAN, base).astype(jnp.int32)


def levels(own_key, shape, pieces, low, largest):
    loudness = 1.0
    for axis_at, shards_of in pieces:
        steps = jax.random.uniform(jax.random.fold_in(jax.random.fold_in(own_key, 6), axis_at), (shards_of,), jnp.float32, low / len(pieces), largest / len(pieces))
        loudness = loudness * jnp.repeat(jnp.exp(steps), shape[axis_at] // shards_of).reshape((-1,) + (1,) * (len(shape) - 1 - axis_at))
    return loudness


def bell_draw(stream_key, dims, width, most, shards=(), held_as=jnp.bfloat16):
    values = jax.random.normal(stream_key, dims, jnp.float32) * width
    if len(shards) > 0:
        values = levels(stream_key, dims, shards, -0.22, 0.18) * values
    return jnp.clip(values, min=-most, max=most).astype(held_as)


def setup_inputs(seed: int = 0) -> dict:
    seeds = jax.random.split(jax.random.key(seed), 21)
    tokens = bell_draw(seeds[0], (BATCH, SPAN, D), 1.0, 6.0, ((0, 8), (1, 4)))
    lengths = draw_lengths(jax.random.fold_in(seeds[20], 71), 0)
    cotangent = bell_draw(seeds[2], (BATCH, SPAN, D), 1.0, 6.0, ((0, 8), (1, 4)))
    w_query = bell_draw(seeds[3], (D, D), D ** -0.5, 0.21875)
    w_key = bell_draw(seeds[4], (D, D), D ** -0.5, 0.21875)
    w_value = bell_draw(seeds[5], (D, D), D ** -0.5, 0.21875)
    w_out = bell_draw(seeds[6], (D, D), (D // 16) ** -0.5, 0.875)
    w_up = bell_draw(seeds[7], (D, FF), D ** -0.5, 0.21875)
    w_down = bell_draw(seeds[8], (FF, D), FF ** -0.5, 0.109375)
    shared_a = bell_draw(seeds[9], (D, RANK), D ** -0.5, 0.21875)
    shared_b = bell_draw(seeds[10], (RANK, D), RANK ** -0.5, 0.1875)
    vec_biases = bell_draw(seeds[11], (6, D), 0.5, 3.0, (), jnp.float32)
    bias_up = bell_draw(seeds[12], (FF,), 0.5, 3.0, (), jnp.float32)
    norm_gains = jnp.clip(1.0 + 0.15 * jax.random.normal(seeds[13], (2, D), jnp.float32), 0.25, 1.75)
    scale_d = bell_draw(seeds[14], (2, RANK), 1.0, 3.0, (), jnp.float32)
    scale_b = bell_draw(seeds[15], (2, D), 1.0, 3.0, (), jnp.float32)
    mom_d = bell_draw(seeds[16], (2, RANK), (0.5 * (BATCH * SPAN) ** 0.5), 384.0, (), jnp.float32)
    sec_d = jnp.clip(jnp.exp(jax.random.uniform(seeds[17], (2, RANK), jnp.float32, math.log(2048.0), math.log(32768.0))), 2048.0, 32768.0)
    mom_b = bell_draw(seeds[18], (2, D), (0.5 * (BATCH * SPAN) ** 0.5), 384.0, (), jnp.float32)
    sec_b = jnp.clip(jnp.exp(jax.random.uniform(seeds[19], (2, D), jnp.float32, math.log(2048.0), math.log(32768.0))), 2048.0, 32768.0)
    return {"tokens": tokens, "lengths": lengths, "cotangent": cotangent, "w_query": w_query, "w_key": w_key, "w_value": w_value, "w_out": w_out, "w_up": w_up, "w_down": w_down, "shared_a": shared_a, "shared_b": shared_b, "vec_biases": vec_biases, "bias_up": bias_up, "norm_gains": norm_gains, "scale_d": scale_d, "scale_b": scale_b, "mom_d": mom_d, "sec_d": sec_d, "mom_b": mom_b, "sec_b": sec_b}


@jax.custom_vjp
def low(v):
    return lax.optimization_barrier(v.astype(jnp.bfloat16)).astype(jnp.float32)

@jax.custom_vjp
def low_back(v):
    return v

def low_keep(v):
    return (low(v), None)

def low_pass(kept, grad):
    return (grad,)

def back_keep(v):
    return (v, None)

def back_low(kept, grad):
    return (low(grad),)
low.defvjp(low_keep, low_pass)
low_back.defvjp(back_keep, back_low)

def matmul(left, right):
    return jnp.dot(left, right, precision=lax.Precision.HIGHEST, preferred_element_type=jnp.float32)

def norm_rows(values, gain, shift):
    centred = values - lax.optimization_barrier(jnp.mean(values, axis=-1, keepdims=True))
    variance = lax.optimization_barrier(jnp.mean(centred * centred, axis=-1, keepdims=True))
    return centred * lax.rsqrt(variance + 1e-05) * gain + shift

def attend(items):
    queries, keys, values, count = items
    scores = jnp.einsum('qhd,khd->qhk', queries, keys, precision=lax.Precision.HIGHEST) * HEAD ** (-0.5)
    scores = low_back(scores)
    usable = jnp.arange(SPAN, dtype=jnp.int32) < count
    scores = jnp.where(usable[None, None, :], scores, -1000000000.0)
    top = lax.optimization_barrier(jnp.max(scores, axis=-1, keepdims=True))
    expo = jnp.exp(scores - top)
    probs = low(expo / lax.optimization_barrier(jnp.sum(expo, axis=-1, keepdims=True)))
    return jnp.einsum('qhk,khd->qhd', probs, values, precision=lax.Precision.HIGHEST)

def adamw(weight, moment, second, gradient):
    moment_new = 0.5 * moment + 0.5 * gradient
    second_new = 0.5 * second + 0.5 * gradient * gradient
    first_hat = moment_new / (1.0 - 0.5 ** STEP)
    second_hat = second_new / (1.0 - 0.5 ** STEP)
    weight_new = weight - 0.25 * (first_hat / (jnp.sqrt(second_hat) + 1e-08) + 0.01 * weight)
    return (moment_new, second_new, weight_new)

def reference(tokens, lengths, cotangent, w_query, w_key, w_value, w_out, w_up, w_down, shared_a, shared_b, vec_biases, bias_up, norm_gains, scale_d, scale_b, mom_d, sec_d, mom_b, sec_b):
    f32 = jnp.float32
    wq, wk, wv, wo = (w_query.astype(f32), w_key.astype(f32), w_value.astype(f32), w_out.astype(f32))
    wup, wdown = (w_up.astype(f32), w_down.astype(f32))
    mat_a, mat_b = (shared_a.astype(f32), shared_b.astype(f32))
    inputs = tokens.astype(f32).reshape(BATCH * SPAN, D)
    positions = jnp.arange(SPAN, dtype=jnp.int32)
    row_mask = (positions[None, :] < lengths[:, None]).astype(f32).reshape(BATCH * SPAN, 1)

    def forward(rows, vec_d, vec_b):
        latent = low_back(matmul(rows, mat_a))
        lat_q = low(latent * vec_d[0])
        lat_v = low(latent * vec_d[1])
        branch_q = low_back(matmul(lat_q, mat_b))
        branch_v = low_back(matmul(lat_v, mat_b))
        queries = low(low_back(matmul(rows, wq) + vec_biases[0] + vec_b[0] * branch_q))
        keys = low(low_back(matmul(rows, wk)))
        values = low(low_back(matmul(rows, wv) + vec_biases[1] + vec_b[1] * branch_v))
        shape4 = (BATCH, SPAN, HEADS, HEAD)
        context = lax.map(jax.checkpoint(attend), (queries.reshape(shape4), keys.reshape(shape4), values.reshape(shape4), lengths))
        context = low(low_back(context.reshape(BATCH * SPAN, D)))
        attn_out = low_back(matmul(context, wo)) + vec_biases[2]
        first = norm_rows(rows + attn_out, norm_gains[0], vec_biases[4])
        pre_act = low_back(matmul(low(first), wup) + bias_up)
        hidden = low(jax.nn.gelu(pre_act, approximate=False))
        ffn_out = low_back(matmul(hidden, wdown)) + vec_biases[3]
        second = norm_rows(first + ffn_out, norm_gains[1], vec_biases[5])
        return second * row_mask
    result, pullback = jax.vjp(forward, inputs, scale_d, scale_b)
    grad_rows, grad_d, grad_b = pullback(cotangent.astype(f32).reshape(BATCH * SPAN, D))
    moment_d, second_d, new_d = adamw(scale_d, mom_d, sec_d, grad_d)
    moment_b, second_b, new_b = adamw(scale_b, mom_b, sec_b, grad_b)
    return (result.reshape(BATCH, SPAN, D).astype(jnp.bfloat16), grad_rows.reshape(BATCH, SPAN, D), moment_d, second_d, moment_b, second_b, new_d, new_b, new_d.astype(jnp.bfloat16), new_b.astype(jnp.bfloat16))
```

```python
from functools import partial

import jax
import jax.numpy as jnp
from jax import lax
from jax.experimental import pallas as pl
from jax.experimental.pallas import tpu as pltpu
from jax.sharding import PartitionSpec as P

HEADS = 12
HEAD = 64
PAIR = 2 * HEAD
ROWS = 16
STEP = 10
EPSILON = 1e-05
LOG2E = 1.4426950408889634
LN2 = 0.6931471805599453
SCORE_SCALE = HEAD ** (-0.5) * LOG2E
MASKED = -1000000000.0 * LOG2E
LEAST, MOST = 2.0**-80, 2.0**100
CHUNK = 32
VMEM_BYTES = 64 * 1024 * 1024 - 128 * 1024

f32 = jnp.float32
bf16 = jnp.bfloat16

VMEM = pl.BlockSpec(memory_space=pltpu.VMEM)
SMEM = pl.BlockSpec(memory_space=pltpu.SMEM)
HBM = pl.BlockSpec(memory_space=pltpu.HBM)
ANY = pl.BlockSpec(memory_space=pl.ANY)


def product(left, right):
    return jnp.dot(left, right, preferred_element_type=f32)


def product_back(left, right):
    return lax.dot_general(left, right, (((1,), (1,)), ((), ())), preferred_element_type=f32)


def adamw(weight, moment, second, gradient):
    moment_new = 0.5 * moment + 0.5 * gradient
    second_new = 0.5 * second + 0.5 * gradient * gradient
    first_hat = moment_new / (1.0 - 0.5**STEP)
    second_hat = second_new / (1.0 - 0.5**STEP)
    weight_new = weight - 0.25 * (first_hat / (jnp.sqrt(second_hat) + 1e-08) + 0.01 * weight)
    return (moment_new, second_new, weight_new)


def shaped(shape, dtype):
    return jax.ShapeDtypeStruct(shape, dtype)


def buffers(*shapes, dtype=bf16):
    return [pltpu.VMEM(shape, dtype) for shape in shapes]


def lanes(shape):
    return lax.broadcasted_iota(jnp.int32, shape, len(shape) - 1)


def half_mask(which):
    return jnp.where(lanes((1, PAIR)) // HEAD == which, 1.0, 0.0).astype(bf16)


def row_chunks(rows, size=CHUNK):
    return [slice(at, at + size) for at in range(0, rows, size)]


def span_of(at, size):
    return pl.ds(pl.multiple_of(at * size, size), size)


def for_each(count, body):
    def step(at, carry):
        body(at)
        return carry

    lax.fori_loop(0, count, step, 0)


def make_copies(pairs, sems):
    return [pltpu.make_async_copy(src, dst, sems.at[n]) for n, (src, dst) in enumerate(pairs)]


def block_start(mask, block):
    return (lax.axis_index("seq") ^ mask) * block


def turned_rows(rows):
    pad = jnp.zeros((PAIR - rows.shape[0], rows.shape[1]), f32)
    return jnp.concatenate([rows, pad], axis=0).T


def call(kernel, name, args, in_specs, outs, scratch, flops, moved, powers=0):
    return pl.pallas_call(
        kernel,
        in_specs=in_specs,
        out_specs=[spec for spec, _, _ in outs],
        out_shape=[shaped(shape, dtype) for _, shape, dtype in outs],
        scratch_shapes=scratch,
        compiler_params=pltpu.CompilerParams(vmem_limit_bytes=VMEM_BYTES),
        cost_estimate=pl.CostEstimate(flops=flops, bytes_accessed=moved, transcendentals=powers),
        name=name,
    )(*args)


def both(rows):
    return rows[...].reshape(2 * rows.shape[1], rows.shape[2])


def project_keys(x, weights, k, kt):
    rows, width = x.shape[1:]
    keys = product(both(x), weights[:, 0:width])
    for block in range(2):
        for at in row_chunks(rows):
            k[block, at, :] = keys[block * rows + at.start : block * rows + at.stop].astype(bf16)
        kt[:, block * rows : (block + 1) * rows] = k[block].T


def project_values(x, weights, bias, v, vt):
    rows, width = x.shape[1:]
    values = product(both(x), weights[:, width : 2 * width])
    for block in range(2):
        for at in row_chunks(rows):
            part = values[block * rows + at.start : block * rows + at.stop]
            v[block, at, :] = (part + bias).astype(bf16)
        vt[:, block * rows : (block + 1) * rows] = v[block].T


def attend_fast(q, k, vt, e, o, l, has_prev, finish):
    rows, width = q.shape
    blocks = k.shape[0]
    ones = jnp.ones((ROWS, blocks * rows), bf16)

    def body(pair):
        span = span_of(pair, PAIR)
        for half in range(2):
            head = 2 * pair + half
            q_own = q[:, span] * half_mask(half)
            for block in range(blocks):
                scores = product_back(q_own, k[block, :, span])
                e[head, :, block * rows : (block + 1) * rows] = jnp.exp2(scores).astype(bf16)
            own = span_of(head, HEAD)
            out = product_back(jnp.concatenate([vt[own, :], ones], axis=0), e[head])
            row = pl.ds(head, 1)
            if has_prev:
                o[own, :] += out[:HEAD]
                l[row, :] += out[HEAD : HEAD + 1]
            else:
                o[own, :] = out[:HEAD]
                l[row, :] = out[HEAD : HEAD + 1]
        finish(pair)

    for_each(width // PAIR, body)


def attend_slow(q, k, vt, e, o, l, m, mb, col, has_prev, finish, starts, count):
    rows, width = q.shape
    blocks = k.shape[0]
    ones = jnp.ones((ROWS, blocks * rows), bf16)

    def body(pair):
        span = span_of(pair, PAIR)

        def one_half(half):
            head = 2 * pair + half

            def group(n):
                at = span_of(n, PAIR)
                q_own = q[at, span] * half_mask(half)
                parts = []
                for block in range(blocks):
                    scores = product_back(q_own, k[block, :, span])
                    position = starts[block] + lanes((PAIR, rows))
                    parts.append(jnp.where(position < count, scores, MASKED))
                top = jnp.max(parts[0], axis=1, keepdims=True)
                for part in parts[1:]:
                    top = jnp.maximum(top, jnp.max(part, axis=1, keepdims=True))
                for block in range(blocks):
                    e[head, at, block * rows : (block + 1) * rows] = jnp.exp2(
                        parts[block] - top
                    ).astype(bf16)
                col[at, :] = jnp.broadcast_to(top, (PAIR, PAIR))

            for_each(rows // PAIR, group)
            own = span_of(head, HEAD)
            row = pl.ds(head, 1)
            out = product_back(jnp.concatenate([vt[own, :], ones], axis=0), e[head])
            top = col[...].T[0:1, :]
            if has_prev:
                old = m[row, :]
                top_new = jnp.maximum(old, top)
                keep = jnp.exp2(old - top_new)
                add = jnp.exp2(top - top_new)
                o[own, :] = o[own, :] * keep + out[:HEAD] * add
                l[row, :] = l[row, :] * keep + out[HEAD : HEAD + 1] * add
                mb[row, :] = top
                m[row, :] = top_new
            else:
                o[own, :] = out[:HEAD]
                l[row, :] = out[HEAD : HEAD + 1]
                m[row, :] = top

        for_each(2, one_half)
        finish(pair)

    for_each(width // PAIR, body)


def attend(covered, q, k, vt, e, o, l, m, mb, col, has_prev, starts, count, finish, restore):
    @pl.when(covered)
    def _():
        attend_fast(q, k, vt, e, o, l, has_prev, finish)

    sums = l[...]
    safe = covered & (jnp.min(sums) > LEAST) & (jnp.max(sums) < MOST)

    @pl.when(jnp.logical_not(safe))
    def _():
        restore()
        attend_slow(q, k, vt, e, o, l, m, mb, col, has_prev, finish, starts, count)

    return safe


def near_kernel(
    count_ref,
    d_ref,
    b_ref,
    bias_ref,
    x_hbm,
    wk_hbm,
    a_hbm,
    sb_hbm,
    wq_hbm,
    wv_hbm,
    x_one_hbm,
    fast_ref,
    l,
    m,
    e_hbm,
    o_hbm,
    q_hbm,
    qt_hbm,
    v_hbm,
    kt_hbm,
    w_all_hbm,
    bt_hbm,
    x,
    a,
    sb,
    w,
    scaled,
    e,
    o,
    q,
    qt,
    k,
    v,
    kt,
    vt,
    w_all,
    bt,
    col,
    sems_in,
    sems_out,
    sems_e,
):
    rows, width = x.shape[1:]
    come = make_copies(
        (
            (x_hbm, x.at[0]),
            (a_hbm, a),
            (sb_hbm, sb),
            (wq_hbm, w.at[0]),
            (wk_hbm, w_all.at[:, pl.ds(width, width)]),
            (wv_hbm, w.at[1]),
            (x_one_hbm, x.at[1]),
        ),
        sems_in,
    )
    for n in (0, 6, 4, 1, 2, 3, 5):
        come[n].start()
    leave = make_copies(
        ((q, q_hbm), (qt, qt_hbm), (v, v_hbm), (kt, kt_hbm), (w_all, w_all_hbm), (bt, bt_hbm), (o, o_hbm)),
        sems_out,
    )
    l[...] = jnp.ones_like(l)
    m[...] = jnp.zeros_like(m)

    def folded(n, w):
        for at in row_chunks(width):
            scaled[at, :] = (a[at, :].astype(f32) * d_ref[n : n + 1, :]).astype(bf16)
        adapter = product(scaled[...], sb[...])
        for at in row_chunks(width):
            out = w[at, :].astype(f32) + adapter[at] * b_ref[n : n + 1, :]
            w_all[at, spans[2 * n]] = out.astype(bf16)

    kv = w_all.at[:, pl.ds(width, 2 * width)]
    for n in (0, 6, 4):
        come[n].wait()
    project_keys(x, kv, k, kt)
    leave[3].start()
    for n in (1, 2, 3, 5):
        come[n].wait()

    def folded(n):
        row = pl.ds(n, 1)
        for at in row_chunks(width):
            scaled[at, :] = (a[at, :].astype(f32) * d_ref[row, :]).astype(bf16)
        adapter = product(scaled[...], sb[...])
        span = span_of(2 * n, width)
        for at in row_chunks(width):
            out = w[n, at, :].astype(f32) + adapter[at] * b_ref[row, :]
            w_all[at, span] = out.astype(bf16)

    for_each(2, folded)
    leave[4].start()
    queries = product(x[0], w_all[:, 0:width])
    for at in row_chunks(rows):
        q[at, :] = ((queries[at] + bias_ref[0:1, :]) * SCORE_SCALE).astype(bf16)
    leave[0].start()
    qt[...] = q[...].T
    leave[1].start()
    bt[...] = sb[...].T
    leave[5].start()
    project_values(x, kv, bias_ref[1:2, :], v, vt)
    leave[2].start()
    count = count_ref[0]
    starts = (block_start(0, rows), block_start(1, rows))
    covered = jnp.maximum(*starts) + rows <= count

    def copy_e(pair):
        heads = pl.ds(2 * pair, 2)
        return pltpu.make_async_copy(e.at[heads], e_hbm.at[heads], sems_e.at[pair])

    def restore():
        @pl.when(covered)
        def _():
            for pair in range(width // PAIR):
                copy_e(pair).wait()

    safe = attend(
        covered, q, k, vt, e, o, l, m, m, col, False, starts, count, lambda pair: copy_e(pair).start(), restore
    )
    fast_ref[0] = jnp.where(safe, 1, 0)
    leave[6].start()
    for copy in leave:
        copy.wait()
    for pair in range(width // PAIR):
        copy_e(pair).wait()


def near(lengths, d, b, biases, x, w_key, shared_a, shared_b, w_query, w_value, x_one):
    rows, width = x.shape
    rank = shared_a.shape[1]
    low, square, expo = (rows, width), (width, width), (HEADS, rows, 2 * rows)
    turned = (width, 2 * rows)
    return call(
        near_kernel,
        "near",
        (lengths, d, b, biases, x, w_key, shared_a, shared_b, w_query, w_value, x_one),
        [SMEM, VMEM, VMEM, VMEM] + [HBM] * 6 + [ANY],
        [
            (SMEM, (1,), jnp.int32),
            (VMEM, (ROWS, rows), f32),
            (VMEM, (ROWS, rows), f32),
            (HBM, expo, bf16),
            (HBM, (width, rows), f32),
            (HBM, low, bf16),
            (HBM, (width, rows), bf16),
            (HBM, (2,) + low, bf16),
            (HBM, turned, bf16),
            (HBM, (width, 3 * width), bf16),
            (HBM, (width, rank), bf16),
        ],
        buffers((2,) + low, (width, rank), (rank, width), (2,) + square, (width, rank), expo)
        + buffers((width, rows), dtype=f32)
        + buffers(low, (width, rows), (2,) + low, (2,) + low, turned, turned)
        + buffers((width, 3 * width), (width, rank))
        + buffers((rows, PAIR), dtype=f32)
        + [
            pltpu.SemaphoreType.DMA((7,)),
            pltpu.SemaphoreType.DMA((7,)),
            pltpu.SemaphoreType.DMA((width // PAIR,)),
        ],
        32 * rows * rows * width + 10 * rows * width * width + 4 * width * rank * width,
        40 * 1024 * 1024,
        2 * HEADS * rows * rows,
    )


def attend_back(
    go, got, qt, less, factor, v, kt, e, gqt, gvts, gkvs, scores, ready, done
):
    rows, width = go.shape
    blocks = len(v)
    lane = lanes((rows, PAIR))

    def body(pair):
        span = span_of(pair, PAIR)
        ready(pair)
        g_values, g_keys = [], []
        for half in range(2):
            head = 2 * pair + half
            left = jnp.concatenate([go[:, span] * half_mask(half), less[...]], axis=1)
            picks = jnp.where(lane // 2 == head, 1.0, 0.0).astype(bf16)
            towards = [
                product_back(left, jnp.concatenate([v[block][:, span], picks], axis=1))
                for block in range(blocks)
            ]
            own = jnp.sum(jnp.where(lane == head, factor[...], 0.0), axis=1, keepdims=True)
            own = jnp.broadcast_to(own, (rows, PAIR)).astype(bf16)
            own = jnp.concatenate([own] * (rows // PAIR), axis=1)
            for block in range(blocks):
                here = slice(block * rows, (block + 1) * rows)
                for at in row_chunks(rows):
                    weights = e[head, at, here] * own[at]
                    e[head, at, here] = weights
                    scores[half, at, here] = weights * towards[block][at].astype(bf16)
            span_own = span_of(head, HEAD)
            g_values.append(product(got[span_own, :], e[head]).astype(bf16))
            g_keys.append((product(qt[span_own, :], scores[half]) * LN2).astype(bf16))
            gqt[span_own, :] += product_back(kt[span_own, :], scores[half])
        g_values = jnp.concatenate(g_values, axis=0)
        g_keys = jnp.concatenate(g_keys, axis=0)
        value_span = pl.ds(pl.multiple_of(width + pair * PAIR, PAIR), PAIR)
        for block in range(blocks):
            here = slice(block * rows, (block + 1) * rows)
            gvts[block][span, :] = g_values[:, here]
            gkvs[block][:, span] = g_keys[:, here].T
            gkvs[block][:, value_span] = g_values[:, here].T
        done(pair)

    for_each(width // PAIR, body)


def norm_parts(values):
    width = values.shape[1]
    centred = values - jnp.sum(values, axis=1, keepdims=True) * (1.0 / width)
    variance = jnp.sum(centred * centred, axis=1, keepdims=True) * (1.0 / width)
    scale = lax.rsqrt(variance + EPSILON)
    return centred * scale, scale


def norm_back(grad, hat, scale):
    width = grad.shape[1]
    mean = jnp.sum(grad, axis=1, keepdims=True) * (1.0 / width)
    along = jnp.sum(grad * hat, axis=1, keepdims=True) * (1.0 / width)
    return scale * (grad - mean - hat * along)


def gelu_pair(x):
    phi = 0.5 + 0.5 * lax.erf(x * 0.7071067811865476)
    bell = jnp.exp2(x * x * (-0.5 * LOG2E))
    return x * phi, phi + x * bell * 0.3989422804014327


def middle(
    count,
    o,
    invt,
    x,
    cot,
    go,
    got,
    acc_ref,
    lesst,
    hat_ref,
    low_ref,
    pool,
    scale_ref,
    bias_ref,
    bias_up_ref,
    gain_ref,
    w_out,
    w_up,
    w_down,
    waits,
    sends,
):
    rows, width = x.shape
    hidden = w_up.shape[1]
    chunk = 512
    slabs = pool.shape[0] // 2
    wide = pool.shape[2]

    def slab_of(start):
        return start // wide, slice(start % wide, start % wide + chunk)


    for head in range(HEADS):
        own = slice(head * HEAD, (head + 1) * HEAD)
        o[own, :] = o[own, :] * invt[head : head + 1, :]
    low_ref[...] = o[...].astype(bf16).T
    waits[0]()
    attn = product(low_ref[...], w_out[...])
    for at in row_chunks(rows):
        hat, scale = norm_parts(x[at, :].astype(f32) + attn[at] + bias_ref[2:3, :])
        scale_ref[at, :] = jnp.broadcast_to(scale, (CHUNK, PAIR))
        hat_ref[at, :] = hat.astype(bf16)
        normed = hat * gain_ref[0:1, :] + bias_ref[4:5, :]
        low_ref[at, :] = normed.astype(bf16)
        acc_ref[at, :] = normed + bias_ref[3:4, :]
    waits[1]()

    for start in range(0, hidden, chunk):
        span = slice(start, start + chunk)
        slab, here = slab_of(start)
        pre = product(low_ref[...], w_up[:, span])
        for at in row_chunks(rows):
            bent, slope = gelu_pair(pre[at] + bias_up_ref[:, span])
            pool[slab, at, here] = bent.astype(bf16)
            pool[slabs + slab, at, here] = slope.astype(bf16)
    waits[2]()

    def slabs_of_pool():
        return jnp.concatenate([pool[slab] for slab in range(slabs)], axis=1)

    ffn = product(slabs_of_pool(), w_down[...])
    waits[3]()
    first = block_start(0, rows)
    for at in row_chunks(rows):
        hat, scale = norm_parts(acc_ref[at, :] + ffn[at])
        position = first + at.start + lax.broadcasted_iota(jnp.int32, (CHUNK, 1), 0)
        valid = jnp.where(position < count, 1.0, 0.0)
        grad = cot[at, :].astype(f32) * gain_ref[1:2, :]
        cot[at, :] = ((hat * gain_ref[1:2, :] + bias_ref[5:6, :]) * valid).astype(bf16)
        g_two = norm_back(grad, hat, scale * valid)
        low_ref[at, :] = g_two.astype(bf16)
        acc_ref[at, :] = g_two
    sends[0]()

    for start in range(0, hidden, chunk):
        slab, here = slab_of(start)
        g_hidden = product_back(low_ref[...], w_down[start : start + chunk, :])
        for at in row_chunks(rows):
            g_pre = g_hidden[at] * pool[slabs + slab, at, here].astype(f32)
            pool[slab, at, here] = g_pre.astype(bf16)
    g_up = product_back(slabs_of_pool(), w_up[...])
    for at in row_chunks(rows):
        grad = (acc_ref[at, :] + g_up[at]) * gain_ref[0:1, :]
        out = norm_back(grad, hat_ref[at, :].astype(f32), scale_ref[at, 0:1])
        acc_ref[at, :] = out
        low_ref[at, :] = out.astype(bf16)
    sends[1]()
    grad_out = product_back(low_ref[...], w_out[...])
    for at in row_chunks(rows):
        go[at, :] = grad_out[at].astype(bf16)
    got[...] = go[...].T
    lesst[...] = jnp.zeros_like(lesst)
    for head in range(HEADS):
        own = slice(head * HEAD, (head + 1) * HEAD)
        delta = jnp.sum(got[own, :].astype(f32) * o[own, :], axis=0, keepdims=True)
        high = delta.astype(bf16).astype(f32)
        lesst[2 * head : 2 * head + 1, :] = -high
        lesst[2 * head + 1 : 2 * head + 2, :] = high - delta


def far_kernel(
    count_ref,
    fast_ref,
    bias_ref,
    bias_up_ref,
    gain_ref,
    d_ref,
    b_ref,
    l_prev,
    m_prev,
    w_all_hbm,
    x_two_hbm,
    x_three_hbm,
    q_hbm,
    o_hbm,
    w_out_hbm,
    w_up_hbm,
    w_down_hbm,
    x_hbm,
    cot_hbm,
    qt_hbm,
    x_one_hbm,
    v_near_hbm,
    kt_near_hbm,
    e_near_hbm,
    a_hbm,
    bt_hbm,
    total_ref,
    act_hbm,
    rest_hbm,
    two_hbm,
    three_hbm,
    one_hbm,
    w_all,
    x_far,
    q,
    o,
    w_out,
    w_up,
    w_down,
    x,
    cot,
    qt,
    g_one,
    got,
    kv,
    turned,
    e,
    pool,
    gkv,
    scores,
    l,
    m,
    mb,
    lesst,
    less,
    factors,
    scale_ref,
    hat_ref,
    sems_in,
    sems_e,
    sems_late,
    sems_out,
):
    rows, width = x.shape
    pairs = width // PAIR
    go, low_ref = q, x_far.at[1]
    come = make_copies(
        (
            (w_all_hbm, w_all),
            (x_two_hbm, x_far.at[0]),
            (x_three_hbm, x_far.at[1]),
            (q_hbm, q),
            (o_hbm, o),
            (w_out_hbm, w_out),
            (x_hbm, x),
            (w_up_hbm, w_up),
            (w_down_hbm, w_down),
            (cot_hbm, cot),
            (qt_hbm, qt),
        ),
        sems_in,
    )
    for copy in come[:3]:
        copy.start()
    v, k = kv.at[pl.ds(0, 2)], kv.at[pl.ds(2, 2)]
    kt, vt = turned.at[0], turned.at[1]
    x_all = w_down.at[pl.ds(0, 4 * rows)]
    a = w_up.at[:, pl.ds(0, 2 * rows)]
    gvt_all = w_up.at[:, pl.ds(2 * rows, 4 * rows)]
    late = make_copies(
        (
            (v_near_hbm, k),
            (kt_near_hbm, vt),
            (x_hbm, x_all.at[pl.ds(0, rows)]),
            (x_one_hbm, x_all.at[pl.ds(rows, rows)]),
            (x_two_hbm, x_all.at[pl.ds(2 * rows, rows)]),
            (x_three_hbm, x_all.at[pl.ds(3 * rows, rows)]),
            (a_hbm, a),
            (bt_hbm, kt),
        ),
        sems_late,
    )
    leave = make_copies(
        (
            (cot, act_hbm),
            (x_far.at[0], two_hbm),
            (x_far.at[1], three_hbm),
            (g_one, rest_hbm),
            (x_far.at[1], one_hbm),
        ),
        sems_out,
    )

    def copy_e(pair):
        heads = pl.ds(2 * pair, 2)
        return pltpu.make_async_copy(e_near_hbm.at[heads], e.at[heads], sems_e.at[pair])

    l[...] = l_prev[...]
    m[...] = m_prev[...]
    mb[...] = jnp.zeros_like(mb)
    wkv = w_all.at[:, pl.ds(width, 2 * width)]
    for copy in come[:3]:
        copy.wait()
    for copy in come[3:]:
        copy.start()
    project_keys(x_far, wkv, k, kt)
    project_values(x_far, wkv, bias_ref[1:2, :], v, vt)
    count = count_ref[0]
    starts = (block_start(2, rows), block_start(3, rows))
    covered = (jnp.maximum(*starts) + rows <= count) & (fast_ref[0] == 1)
    come[3].wait()
    come[4].wait()

    def restore():
        l[...] = l_prev[...]
        again = pltpu.make_async_copy(o_hbm, o, sems_in.at[4])
        again.start()
        again.wait()

    col = factors.at[0]
    attend(covered, q, k, vt, e, o, l, m, mb, col, True, starts, count, lambda pair: None, restore)
    for copy in late[:2]:
        copy.start()

    invt = 1.0 / l[...]
    factors[0] = turned_rows(invt * jnp.exp2(mb[...] - m[...]))
    factors[1] = turned_rows(invt * jnp.exp2(m_prev[...] - m[...]))

    def waits(*which):
        def wait():
            for n in which:
                come[n].wait()

        return wait

    def fetch_late():
        for copy in late[2:7]:
            copy.start()

    middle(
        count,
        o,
        invt,
        x,
        cot,
        go,
        got,
        g_one,
        lesst,
        hat_ref,
        low_ref,
        pool,
        scale_ref,
        bias_ref,
        bias_up_ref,
        gain_ref,
        w_out,
        w_up,
        w_down,
        (waits(5, 6), waits(7), waits(8), waits(9, 10)),
        (leave[0].start, fetch_late),
    )
    less[...] = lesst[...].T.astype(bf16)
    o[...] = jnp.zeros_like(o)

    def one_chip(chip):
        own = chip == 1

        @pl.when(own)
        def _():
            late[0].wait()
            late[1].wait()

        def ready(pair):
            @pl.when(own)
            def _():
                copy_e(pair).wait()

        def done(pair):
            @pl.when(jnp.logical_not(own))
            def _():
                copy_e(pair).start()

        attend_back(
            go,
            got,
            qt,
            less,
            factors.at[chip],
            [kv.at[2 * chip + block] for block in range(2)],
            turned.at[chip],
            e,
            o,
            [gvt_all.at[:, span_of(2 - 2 * chip + block, rows)] for block in range(2)],
            (gkv.at[0], gkv.at[1]),
            scores,
            ready,
            done,
        )

        @pl.when(own)
        def _():
            leave[1].wait()
            leave[2].wait()

        out = product_back(both(gkv), wkv[...])
        for block in range(2):
            for at in row_chunks(rows):
                part = out[block * rows + at.start : block * rows + at.stop]
                x_far[block, at, :] = part.astype(bf16)

        @pl.when(own)
        def _():
            leave[4].start()

        @pl.when(jnp.logical_not(own))
        def _():
            leave[1].start()
            leave[2].start()
            late[7].start()

    for_each(2, one_chip)
    for at in row_chunks(width):
        got[at, :] = (o[at, :] * HEAD ** (-0.5)).astype(bf16)
    go[...] = got[...].T
    out = product_back(go[...], w_all[:, 0:width])
    for at in row_chunks(rows):
        g_one[at, :] += out[at] + x_far[0, at, :].astype(f32)
    leave[3].start()
    for copy in late[2:]:
        copy.wait()
    bt = kt
    rank = a.shape[1]
    total_ref[...] = jnp.zeros_like(total_ref)
    eye = lax.broadcasted_iota(jnp.int32, (PAIR, PAIR), 0) == lanes((PAIR, PAIR))
    for n in range(2):
        if n == 0:
            outer = product(got[...], x_all[0:rows, :])
        else:
            outer = product(gvt_all[...], x_all[...])
        mixed = product(outer.astype(bf16), a[...])
        for_d = jnp.zeros((1, rank), f32)
        for at in row_chunks(width, PAIR):
            part = mixed[at] * bt[at, :].astype(f32)
            column = jnp.sum(jnp.where(eye, b_ref[n : n + 1, at], 0.0), axis=1, keepdims=True)
            for_d = for_d + jnp.sum(part * column, axis=0, keepdims=True)
            sums = jnp.sum(part * d_ref[n : n + 1, :], axis=1, keepdims=True)
            total_ref[2 + n : 3 + n, at] = jnp.sum(jnp.where(eye, sums, 0.0), axis=0, keepdims=True)
        total_ref[n : n + 1, :] = for_d
    for copy in (leave[0], leave[3], leave[4]):
        copy.wait()


def far(small, large):
    w_all, x_two, x_three, q, o, w_out, w_up, w_down = large[:8]
    a = large[-2]
    rows, width = x_two.shape
    hidden = w_up.shape[1]
    rank = a.shape[1]
    low, square, expo = (rows, width), (width, width), (HEADS, rows, 2 * rows)
    turned, row, stat = (width, 2 * rows), (ROWS, rows), (rows, PAIR)
    flat = (width, rows)
    places = [HBM, ANY, ANY] + [HBM] * (len(large) - 3)
    places[11] = ANY
    return call(
        far_kernel,
        "far",
        (*small, *large),
        [SMEM] * 2 + [VMEM] * (len(small) - 2) + places,
        [
            (VMEM, (4, rank), f32),
            (HBM, low, bf16),
            (HBM, low, f32),
            (HBM, low, bf16),
            (HBM, low, bf16),
            (HBM, low, bf16),
        ],
        buffers((width, 3 * width), (2,) + low, low)
        + buffers(flat, dtype=f32)
        + buffers(square, (width, hidden), (hidden, width), low, low, flat)
        + buffers(low, dtype=f32)
        + buffers(flat, (4,) + low, (2,) + turned, expo)
        + buffers((2 * hidden // (2 * rows), rows, 2 * rows))
        + buffers((2, rows, 2 * width), (2, rows, 2 * rows))
        + buffers(row, row, row, (PAIR, rows), dtype=f32)
        + buffers(stat)
        + buffers((2,) + stat, stat, dtype=f32)
        + buffers(low)
        + [
            pltpu.SemaphoreType.DMA((11,)),
            pltpu.SemaphoreType.DMA((width // PAIR,)),
            pltpu.SemaphoreType.DMA((8,)),
            pltpu.SemaphoreType.DMA((5,)),
        ],
        160 * rows * rows * width + 30 * rows * width * width + 8 * rows * width * hidden,
        60 * 1024 * 1024,
        2 * HEADS * rows * rows + 2 * rows * hidden,
    )


def tree_sum(terms):
    while len(terms) > 1:
        terms = [terms[n] + terms[n + 1] for n in range(0, len(terms), 2)]
    return terms[0]


def step_kernel(count, *refs):
    totals = tree_sum([ref[...] for ref in refs[:count]])
    weights = refs[count : count + 6]
    outs = refs[count + 6 :]
    for n in range(2):
        weight, moment, second = weights[3 * n : 3 * n + 3]
        grad = totals[2 * n : 2 * n + 2, : weight.shape[1]]
        moment_new, second_new, weight_new = adamw(weight[...], moment[...], second[...], grad)
        outs[2 * n][...] = moment_new
        outs[2 * n + 1][...] = second_new
        outs[4 + n][...] = weight_new
        outs[6 + n][...] = weight_new.astype(bf16)


def step(terms, weights):
    d, b = weights[0].shape, weights[3].shape
    shapes = [(s, f32) for s in (d, d, b, b, d, b)] + [(d, bf16), (b, bf16)]
    return pl.pallas_call(
        partial(step_kernel, len(terms)),
        in_specs=[VMEM] * (len(terms) + 6),
        out_specs=[VMEM] * 8,
        out_shape=[shaped(*one) for one in shapes],
        name="step",
    )(*terms, *weights)


def swap(value, axis, size, mask):
    return lax.ppermute(value, axis, [(i, i ^ mask) for i in range(size)])


def partners(value, axis, size, stride):
    radix = min(4, size // stride)
    return [value] + [swap(value, axis, size, n * stride) for n in range(1, radix)]


def per_device(
    seq_size,
    dp_size,
    tokens,
    lengths,
    cotangent,
    w_query,
    w_key,
    w_value,
    w_out,
    w_up,
    w_down,
    shared_a,
    shared_b,
    vec_biases,
    bias_up,
    norm_gains,
    scale_d,
    scale_b,
    mom_d,
    sec_d,
    mom_b,
    sec_b,
):
    _, local_len, width = tokens.shape
    x = tokens.reshape(local_len, width)
    x_one = swap(x, "seq", seq_size, 1)
    x_two = swap(x, "seq", seq_size, 2)
    fast, l, m, e_near, o, q, qt, v_near, kt_near, w_all, b_turned = near(
        lengths, scale_d, scale_b, vec_biases, x, w_key, shared_a, shared_b, w_query, w_value, x_one
    )
    x_two, o = lax.optimization_barrier((x_two, o))
    x_three = swap(x_two, "seq", seq_size, 1)
    totals, activations, rest, two, three, one = far(
        (
            lengths,
            fast,
            vec_biases,
            bias_up.reshape(1, -1),
            norm_gains,
            scale_d,
            scale_b,
            l,
            m,
        ),
        (
            w_all,
            x_two,
            x_three,
            q,
            o,
            w_out,
            w_up,
            w_down,
            x,
            cotangent.reshape(local_len, width),
            qt,
            x_one,
            v_near,
            kt_near,
            e_near,
            shared_a,
            b_turned,
        ),
    )
    from_three = swap(three, "seq", seq_size, 1)
    joined = (two.astype(f32) + from_three.astype(f32)).astype(bf16)
    terms = partners(totals, "seq", seq_size, 1)
    joined, *terms = lax.optimization_barrier((joined, *terms))
    from_two = swap(joined, "seq", seq_size, 2)
    from_one = swap(one, "seq", seq_size, 1)
    stride = 1
    while stride < dp_size:
        terms = partners(tree_sum(terms), "dp", dp_size, stride)
        stride *= len(terms)
    moment_d, second_d, moment_b, second_b, new_d, new_b, copy_d, copy_b = step(
        terms, (scale_d, mom_d, sec_d, scale_b, mom_b, sec_b)
    )
    grad_inputs = rest + from_one.astype(f32) + from_two.astype(f32)
    return (
        activations.reshape(tokens.shape),
        grad_inputs.reshape(tokens.shape),
        moment_d,
        second_d,
        moment_b,
        second_b,
        new_d,
        new_b,
        copy_d,
        copy_b,
    )


def solution(mesh):
    rows = P("dp", "seq", None)
    return jax.shard_map(
        partial(per_device, mesh.shape["seq"], mesh.shape["dp"]),
        mesh=mesh,
        in_specs=(rows, P("dp"), rows) + (P(),) * 17,
        out_specs=(rows, rows) + (P(),) * 8,
        check_vma=False,
    )
```

```python
from functools import partial

import jax
import jax.numpy as jnp
from jax import lax
from jax.experimental import pallas as pl
from jax.experimental.pallas import tpu as pltpu
from jax.sharding import PartitionSpec as P

HEADS = 12
HEAD = 64
PAIR = 2 * HEAD
ROWS = 16
STEP = 10
EPSILON = 1e-05
LOG2E = 1.4426950408889634
LN2 = 0.6931471805599453
SCORE_SCALE = HEAD ** (-0.5) * LOG2E
MASKED = -1000000000.0 * LOG2E
LEAST, MOST = 2.0**-80, 2.0**100
CHUNK = 32
VMEM_BYTES = 64 * 1024 * 1024 - 128 * 1024

f32 = jnp.float32
bf16 = jnp.bfloat16

VMEM = pl.BlockSpec(memory_space=pltpu.VMEM)
SMEM = pl.BlockSpec(memory_space=pltpu.SMEM)
HBM = pl.BlockSpec(memory_space=pltpu.HBM)
ANY = pl.BlockSpec(memory_space=pl.ANY)


def product(left, right):
    return jnp.dot(left, right, preferred_element_type=f32)


def product_back(left, right):
    return lax.dot_general(left, right, (((1,), (1,)), ((), ())), preferred_element_type=f32)


def adamw(weight, moment, second, gradient):
    moment_new = 0.5 * moment + 0.5 * gradient
    second_new = 0.5 * second + 0.5 * gradient * gradient
    first_hat = moment_new / (1.0 - 0.5**STEP)
    second_hat = second_new / (1.0 - 0.5**STEP)
    weight_new = weight - 0.25 * (first_hat / (jnp.sqrt(second_hat) + 1e-08) + 0.01 * weight)
    return (moment_new, second_new, weight_new)


def shaped(shape, dtype):
    return jax.ShapeDtypeStruct(shape, dtype)


def buffers(*shapes, dtype=bf16):
    return [pltpu.VMEM(shape, dtype) for shape in shapes]


def lanes(shape):
    return lax.broadcasted_iota(jnp.int32, shape, len(shape) - 1)


def half_mask(which):
    return jnp.where(lanes((1, PAIR)) // HEAD == which, 1.0, 0.0).astype(bf16)


def row_chunks(rows, size=CHUNK):
    return [slice(at, at + size) for at in range(0, rows, size)]


def span_of(at, size):
    return pl.ds(pl.multiple_of(at * size, size), size)


def for_each(count, body):
    def step(at, carry):
        body(at)
        return carry

    lax.fori_loop(0, count, step, 0)


def make_copies(pairs, sems):
    return [pltpu.make_async_copy(src, dst, sems.at[n]) for n, (src, dst) in enumerate(pairs)]


def block_start(mask, block):
    return (lax.axis_index("seq") ^ mask) * block


def turned_rows(rows):
    pad = jnp.zeros((PAIR - rows.shape[0], rows.shape[1]), f32)
    return jnp.concatenate([rows, pad], axis=0).T


def call(kernel, name, args, in_specs, outs, scratch, flops, moved, powers=0):
    return pl.pallas_call(
        kernel,
        in_specs=in_specs,
        out_specs=[spec for spec, _, _ in outs],
        out_shape=[shaped(shape, dtype) for _, shape, dtype in outs],
        scratch_shapes=scratch,
        compiler_params=pltpu.CompilerParams(vmem_limit_bytes=VMEM_BYTES),
        cost_estimate=pl.CostEstimate(flops=flops, bytes_accessed=moved, transcendentals=powers),
        name=name,
    )(*args)


def both(rows):
    return rows[...].reshape(2 * rows.shape[1], rows.shape[2])


def project_keys(x, weights, k, kt):
    rows, width = x.shape[1:]
    keys = product(both(x), weights[:, 0:width])
    for block in range(2):
        for at in row_chunks(rows):
            k[block, at, :] = keys[block * rows + at.start : block * rows + at.stop].astype(bf16)
        kt[:, block * rows : (block + 1) * rows] = k[block].T


def project_values(x, weights, bias, v, vt):
    rows, width = x.shape[1:]
    values = product(both(x), weights[:, width : 2 * width])
    for block in range(2):
        for at in row_chunks(rows):
            part = values[block * rows + at.start : block * rows + at.stop]
            v[block, at, :] = (part + bias).astype(bf16)
        vt[:, block * rows : (block + 1) * rows] = v[block].T


def attend_fast(q, k, vt, e, o, l, has_prev, finish):
    rows, width = q.shape
    blocks = k.shape[0]
    ones = jnp.ones((ROWS, blocks * rows), bf16)

    def body(pair):
        span = span_of(pair, PAIR)
        for half in range(2):
            head = 2 * pair + half
            keys = k[:, :, span].reshape(blocks * rows, PAIR)
            scores = product_back(q[:, span] * half_mask(half), keys)
            for at in row_chunks(rows):
                e[head, at, :] = jnp.exp2(scores[at]).astype(bf16)
            own = span_of(head, HEAD)
            out = product_back(jnp.concatenate([vt[own, :], ones], axis=0), e[head])
            row = pl.ds(head, 1)
            if has_prev:
                o[own, :] += out[:HEAD]
                l[row, :] += out[HEAD : HEAD + 1]
            else:
                o[own, :] = out[:HEAD]
                l[row, :] = out[HEAD : HEAD + 1]
        finish(pair)

    for_each(width // PAIR, body)


def attend_slow(q, k, vt, e, o, l, m, mb, col, has_prev, finish, starts, count):
    rows, width = q.shape
    blocks = k.shape[0]
    ones = jnp.ones((ROWS, blocks * rows), bf16)

    def body(pair):
        span = span_of(pair, PAIR)

        def one_half(half):
            head = 2 * pair + half

            def group(n):
                at = span_of(n, PAIR)
                q_own = q[at, span] * half_mask(half)
                parts = []
                for block in range(blocks):
                    scores = product_back(q_own, k[block, :, span])
                    position = starts[block] + lanes((PAIR, rows))
                    parts.append(jnp.where(position < count, scores, MASKED))
                top = jnp.max(parts[0], axis=1, keepdims=True)
                for part in parts[1:]:
                    top = jnp.maximum(top, jnp.max(part, axis=1, keepdims=True))
                for block in range(blocks):
                    e[head, at, block * rows : (block + 1) * rows] = jnp.exp2(
                        parts[block] - top
                    ).astype(bf16)
                col[at, :] = jnp.broadcast_to(top, (PAIR, PAIR))

            for_each(rows // PAIR, group)
            own = span_of(head, HEAD)
            row = pl.ds(head, 1)
            out = product_back(jnp.concatenate([vt[own, :], ones], axis=0), e[head])
            top = col[...].T[0:1, :]
            if has_prev:
                old = m[row, :]
                top_new = jnp.maximum(old, top)
                keep = jnp.exp2(old - top_new)
                add = jnp.exp2(top - top_new)
                o[own, :] = o[own, :] * keep + out[:HEAD] * add
                l[row, :] = l[row, :] * keep + out[HEAD : HEAD + 1] * add
                mb[row, :] = top
                m[row, :] = top_new
            else:
                o[own, :] = out[:HEAD]
                l[row, :] = out[HEAD : HEAD + 1]
                m[row, :] = top

        for_each(2, one_half)
        finish(pair)

    for_each(width // PAIR, body)


def attend(covered, q, k, vt, e, o, l, m, mb, col, has_prev, starts, count, finish, restore):
    @pl.when(covered)
    def _():
        attend_fast(q, k, vt, e, o, l, has_prev, finish)

    sums = l[...]
    safe = covered & (jnp.min(sums) > LEAST) & (jnp.max(sums) < MOST)

    @pl.when(jnp.logical_not(safe))
    def _():
        restore()
        attend_slow(q, k, vt, e, o, l, m, mb, col, has_prev, finish, starts, count)

    return safe


def near_kernel(
    count_ref,
    d_ref,
    b_ref,
    bias_ref,
    x_hbm,
    wk_hbm,
    a_hbm,
    sb_hbm,
    wq_hbm,
    wv_hbm,
    x_one_hbm,
    fast_ref,
    l,
    m,
    e_hbm,
    o_hbm,
    q_hbm,
    qt_hbm,
    v_hbm,
    kt_hbm,
    w_all_hbm,
    bt_hbm,
    x,
    a,
    sb,
    w,
    scaled,
    e,
    o,
    q,
    qt,
    k,
    v,
    kt,
    vt,
    w_all,
    bt,
    col,
    sems_in,
    sems_out,
    sems_e,
    sems_o,
):
    rows, width = x.shape[1:]
    come = make_copies(
        (
            (x_hbm, x.at[0]),
            (a_hbm, a),
            (sb_hbm, sb),
            (wq_hbm, w.at[0]),
            (wk_hbm, w_all.at[:, pl.ds(width, width)]),
            (wv_hbm, w.at[1]),
            (x_one_hbm, x.at[1]),
        ),
        sems_in,
    )
    for n in (0, 6, 4, 1, 2, 3, 5):
        come[n].start()
    leave = make_copies(
        ((q, q_hbm), (qt, qt_hbm), (v, v_hbm), (kt, kt_hbm), (w_all, w_all_hbm), (bt, bt_hbm)),
        sems_out,
    )
    l[...] = jnp.ones_like(l)
    m[...] = jnp.zeros_like(m)

    def folded(n, w):
        for at in row_chunks(width):
            scaled[at, :] = (a[at, :].astype(f32) * d_ref[n : n + 1, :]).astype(bf16)
        adapter = product(scaled[...], sb[...])
        for at in row_chunks(width):
            out = w[at, :].astype(f32) + adapter[at] * b_ref[n : n + 1, :]
            w_all[at, spans[2 * n]] = out.astype(bf16)

    kv = w_all.at[:, pl.ds(width, 2 * width)]
    for n in (0, 6, 4):
        come[n].wait()
    project_keys(x, kv, k, kt)
    leave[3].start()
    for n in (1, 2, 3, 5):
        come[n].wait()

    def folded(n):
        row = pl.ds(n, 1)
        for at in row_chunks(width):
            scaled[at, :] = (a[at, :].astype(f32) * d_ref[row, :]).astype(bf16)
        adapter = product(scaled[...], sb[...])
        span = span_of(2 * n, width)
        for at in row_chunks(width):
            out = w[n, at, :].astype(f32) + adapter[at] * b_ref[row, :]
            w_all[at, span] = out.astype(bf16)

    for_each(2, folded)
    leave[4].start()
    queries = product(x[0], w_all[:, 0:width])
    for at in row_chunks(rows):
        q[at, :] = ((queries[at] + bias_ref[0:1, :]) * SCORE_SCALE).astype(bf16)
    leave[0].start()
    qt[...] = q[...].T
    leave[1].start()
    bt[...] = sb[...].T
    leave[5].start()
    project_values(x, kv, bias_ref[1:2, :], v, vt)
    leave[2].start()
    count = count_ref[0]
    starts = (block_start(0, rows), block_start(1, rows))
    covered = jnp.maximum(*starts) + rows <= count

    def copy_e(pair):
        heads = pl.ds(2 * pair, 2)
        return pltpu.make_async_copy(e.at[heads], e_hbm.at[heads], sems_e.at[pair])

    def copy_o(pair):
        span = span_of(pair, PAIR)
        return pltpu.make_async_copy(o.at[span], o_hbm.at[span], sems_o.at[pair])

    def send(pair):
        copy_e(pair).start()
        copy_o(pair).start()

    def restore():
        @pl.when(covered)
        def _():
            for pair in range(width // PAIR):
                copy_e(pair).wait()
                copy_o(pair).wait()

    safe = attend(
        covered, q, k, vt, e, o, l, m, m, col, False, starts, count, send, restore
    )
    fast_ref[0] = jnp.where(safe, 1, 0)
    for copy in leave:
        copy.wait()
    for pair in range(width // PAIR):
        copy_e(pair).wait()
        copy_o(pair).wait()


def near(lengths, d, b, biases, x, w_key, shared_a, shared_b, w_query, w_value, x_one):
    rows, width = x.shape
    rank = shared_a.shape[1]
    low, square, expo = (rows, width), (width, width), (HEADS, rows, 2 * rows)
    turned = (width, 2 * rows)
    return call(
        near_kernel,
        "near",
        (lengths, d, b, biases, x, w_key, shared_a, shared_b, w_query, w_value, x_one),
        [SMEM, VMEM, VMEM, VMEM] + [HBM] * 6 + [ANY],
        [
            (SMEM, (1,), jnp.int32),
            (VMEM, (ROWS, rows), f32),
            (VMEM, (ROWS, rows), f32),
            (HBM, expo, bf16),
            (HBM, (width, rows), f32),
            (HBM, low, bf16),
            (HBM, (width, rows), bf16),
            (HBM, (2,) + low, bf16),
            (HBM, turned, bf16),
            (HBM, (width, 3 * width), bf16),
            (HBM, (width, rank), bf16),
        ],
        buffers((2,) + low, (width, rank), (rank, width), (2,) + square, (width, rank), expo)
        + buffers((width, rows), dtype=f32)
        + buffers(low, (width, rows), (2,) + low, (2,) + low, turned, turned)
        + buffers((width, 3 * width), (width, rank))
        + buffers((rows, PAIR), dtype=f32)
        + [
            pltpu.SemaphoreType.DMA((7,)),
            pltpu.SemaphoreType.DMA((6,)),
            pltpu.SemaphoreType.DMA((width // PAIR,)),
            pltpu.SemaphoreType.DMA((width // PAIR,)),
        ],
        32 * rows * rows * width + 10 * rows * width * width + 4 * width * rank * width,
        40 * 1024 * 1024,
        2 * HEADS * rows * rows,
    )


def attend_back(
    go, got, qt, less, factor, v, kt, e, gqt, gvts, gkvs, scores, ready, done
):
    rows, width = go.shape
    blocks = v.shape[0]
    lane = lanes((blocks * rows, PAIR))
    row_lane = lanes((rows, PAIR))

    def body(pair):
        span = span_of(pair, PAIR)
        ready(pair)
        g_values, g_keys = [], []
        for half in range(2):
            head = 2 * pair + half
            left = jnp.concatenate([go[:, span] * half_mask(half), less[...]], axis=1)
            picks = jnp.where(lane // 2 == head, 1.0, 0.0).astype(bf16)
            values = v[:, :, span].reshape(blocks * rows, PAIR)
            towards = product_back(left, jnp.concatenate([values, picks], axis=1))
            own = jnp.sum(jnp.where(row_lane == head, factor[...], 0.0), axis=1, keepdims=True)
            own = jnp.broadcast_to(own, (rows, PAIR)).astype(bf16)
            own = jnp.concatenate([own] * (blocks * rows // PAIR), axis=1)
            for at in row_chunks(rows):
                weights = e[head, at, :] * own[at]
                e[head, at, :] = weights
                scores[half, at, :] = weights * towards[at].astype(bf16)
            span_own = span_of(head, HEAD)
            g_values.append(product(got[span_own, :], e[head]).astype(bf16))
            g_keys.append((product(qt[span_own, :], scores[half]) * LN2).astype(bf16))
            gqt[span_own, :] += product_back(kt[span_own, :], scores[half])
        g_values = jnp.concatenate(g_values, axis=0)
        g_keys = jnp.concatenate(g_keys, axis=0)
        value_span = pl.ds(pl.multiple_of(width + pair * PAIR, PAIR), PAIR)
        for block in range(blocks):
            here = slice(block * rows, (block + 1) * rows)
            gvts[block][span, :] = g_values[:, here]
            gkvs[block][:, span] = g_keys[:, here].T
            gkvs[block][:, value_span] = g_values[:, here].T
        done(pair)

    for_each(width // PAIR, body)


def norm_parts(values):
    width = values.shape[1]
    centred = values - jnp.sum(values, axis=1, keepdims=True) * (1.0 / width)
    variance = jnp.sum(centred * centred, axis=1, keepdims=True) * (1.0 / width)
    scale = lax.rsqrt(variance + EPSILON)
    return centred * scale, scale


def norm_back(grad, hat, scale):
    width = grad.shape[1]
    mean = jnp.sum(grad, axis=1, keepdims=True) * (1.0 / width)
    along = jnp.sum(grad * hat, axis=1, keepdims=True) * (1.0 / width)
    return scale * (grad - mean - hat * along)


def gelu_pair(x):
    phi = 0.5 + 0.5 * lax.erf(x * 0.7071067811865476)
    bell = jnp.exp2(x * x * (-0.5 * LOG2E))
    return x * phi, phi + x * bell * 0.3989422804014327


def middle(
    count,
    o,
    invt,
    x,
    cot,
    go,
    got,
    acc_ref,
    lesst,
    hat_ref,
    low_ref,
    pool,
    scale_ref,
    bias_ref,
    bias_up_ref,
    gain_ref,
    w_out,
    w_up,
    w_down,
    waits,
    sends,
):
    rows, width = x.shape
    hidden = w_up.shape[1]
    chunk = 512
    slabs = pool.shape[0] // 2
    wide = pool.shape[2]

    def slab_of(start):
        return start // wide, slice(start % wide, start % wide + chunk)


    for head in range(HEADS):
        own = slice(head * HEAD, (head + 1) * HEAD)
        o[own, :] = o[own, :] * invt[head : head + 1, :]
    low_ref[...] = o[...].astype(bf16).T
    waits[0]()
    attn = product(low_ref[...], w_out[...])
    for at in row_chunks(rows):
        hat, scale = norm_parts(x[at, :].astype(f32) + attn[at] + bias_ref[2:3, :])
        scale_ref[at, :] = jnp.broadcast_to(scale, (CHUNK, PAIR))
        hat_ref[at, :] = hat.astype(bf16)
        normed = hat * gain_ref[0:1, :] + bias_ref[4:5, :]
        low_ref[at, :] = normed.astype(bf16)
        acc_ref[at, :] = normed + bias_ref[3:4, :]
    waits[1]()

    for start in range(0, hidden, chunk):
        span = slice(start, start + chunk)
        slab, here = slab_of(start)
        pre = product(low_ref[...], w_up[:, span])
        for at in row_chunks(rows):
            bent, slope = gelu_pair(pre[at] + bias_up_ref[:, span])
            pool[slab, at, here] = bent.astype(bf16)
            pool[slabs + slab, at, here] = slope.astype(bf16)
    waits[2]()

    def slabs_of_pool():
        return jnp.concatenate([pool[slab] for slab in range(slabs)], axis=1)

    ffn = product(slabs_of_pool(), w_down[...])
    waits[3]()
    first = block_start(0, rows)
    for at in row_chunks(rows):
        hat, scale = norm_parts(acc_ref[at, :] + ffn[at])
        position = first + at.start + lax.broadcasted_iota(jnp.int32, (CHUNK, 1), 0)
        valid = jnp.where(position < count, 1.0, 0.0)
        grad = cot[at, :].astype(f32) * gain_ref[1:2, :]
        cot[at, :] = ((hat * gain_ref[1:2, :] + bias_ref[5:6, :]) * valid).astype(bf16)
        g_two = norm_back(grad, hat, scale * valid)
        low_ref[at, :] = g_two.astype(bf16)
        acc_ref[at, :] = g_two
    sends[0]()

    for start in range(0, hidden, chunk):
        slab, here = slab_of(start)
        g_hidden = product_back(low_ref[...], w_down[start : start + chunk, :])
        for at in row_chunks(rows):
            g_pre = g_hidden[at] * pool[slabs + slab, at, here].astype(f32)
            pool[slab, at, here] = g_pre.astype(bf16)
    g_up = product_back(slabs_of_pool(), w_up[...])
    for at in row_chunks(rows):
        grad = (acc_ref[at, :] + g_up[at]) * gain_ref[0:1, :]
        out = norm_back(grad, hat_ref[at, :].astype(f32), scale_ref[at, 0:1])
        acc_ref[at, :] = out
        low_ref[at, :] = out.astype(bf16)
    sends[1]()
    grad_out = product_back(low_ref[...], w_out[...])
    for at in row_chunks(rows):
        go[at, :] = grad_out[at].astype(bf16)
    got[...] = go[...].T
    lesst[...] = jnp.zeros_like(lesst)
    for head in range(HEADS):
        own = slice(head * HEAD, (head + 1) * HEAD)
        delta = jnp.sum(got[own, :].astype(f32) * o[own, :], axis=0, keepdims=True)
        high = delta.astype(bf16).astype(f32)
        lesst[2 * head : 2 * head + 1, :] = -high
        lesst[2 * head + 1 : 2 * head + 2, :] = high - delta


def far_kernel(
    count_ref,
    fast_ref,
    bias_ref,
    bias_up_ref,
    gain_ref,
    d_ref,
    b_ref,
    l_prev,
    m_prev,
    w_all_hbm,
    x_two_hbm,
    x_three_hbm,
    q_hbm,
    o_hbm,
    w_out_hbm,
    w_up_hbm,
    w_down_hbm,
    x_hbm,
    cot_hbm,
    qt_hbm,
    x_one_hbm,
    v_near_hbm,
    kt_near_hbm,
    e_near_hbm,
    a_hbm,
    bt_hbm,
    total_ref,
    act_hbm,
    g_one_hbm,
    two_hbm,
    three_hbm,
    one_hbm,
    gq_hbm,
    wkv,
    x_far,
    q,
    o,
    w_out,
    w_up,
    w_down,
    x,
    cot,
    qt,
    g_one,
    got,
    kv,
    turned,
    e,
    pool,
    gkv,
    scores,
    l,
    m,
    mb,
    lesst,
    less,
    factors,
    scale_ref,
    hat_ref,
    sems_in,
    sems_e,
    sems_late,
    sems_out,
):
    rows, width = x.shape
    pairs = width // PAIR
    go, low_ref = q, x_far.at[1]
    come = make_copies(
        (
            (w_all_hbm.at[:, pl.ds(width, 2 * width)], wkv),
            (x_two_hbm, x_far.at[0]),
            (x_three_hbm, x_far.at[1]),
            (q_hbm, q),
            (o_hbm, o),
            (w_out_hbm, w_out),
            (x_hbm, x),
            (w_up_hbm, w_up),
            (w_down_hbm, w_down),
            (cot_hbm, cot),
            (qt_hbm, qt),
        ),
        sems_in,
    )
    for copy in come[:3]:
        copy.start()
    v, k = kv.at[pl.ds(0, 2)], kv.at[pl.ds(2, 2)]
    kt, vt = turned.at[0], turned.at[1]
    x_all = w_down.at[pl.ds(0, 4 * rows)]
    a = w_up.at[:, pl.ds(0, 2 * rows)]
    gvt_all = w_up.at[:, pl.ds(2 * rows, 4 * rows)]
    late = make_copies(
        (
            (v_near_hbm, k),
            (kt_near_hbm, vt),
            (x_hbm, x_all.at[pl.ds(0, rows)]),
            (x_one_hbm, x_all.at[pl.ds(rows, rows)]),
            (x_two_hbm, x_all.at[pl.ds(2 * rows, rows)]),
            (x_three_hbm, x_all.at[pl.ds(3 * rows, rows)]),
            (a_hbm, a),
            (bt_hbm, kt),
        ),
        sems_late,
    )
    leave = make_copies(
        (
            (cot, act_hbm),
            (x_far.at[0], two_hbm),
            (x_far.at[1], three_hbm),
            (g_one, g_one_hbm),
            (x_far.at[1], one_hbm),
            (go, gq_hbm),
        ),
        sems_out,
    )

    def copy_e(pair):
        heads = pl.ds(2 * pair, 2)
        return pltpu.make_async_copy(e_near_hbm.at[heads], e.at[heads], sems_e.at[pair])

    l[...] = l_prev[...]
    m[...] = m_prev[...]
    mb[...] = jnp.zeros_like(mb)
    for copy in come[:3]:
        copy.wait()
    for copy in come[3:]:
        copy.start()
    project_keys(x_far, wkv, k, kt)
    project_values(x_far, wkv, bias_ref[1:2, :], v, vt)
    count = count_ref[0]
    starts = (block_start(2, rows), block_start(3, rows))
    covered = (jnp.maximum(*starts) + rows <= count) & (fast_ref[0] == 1)
    come[3].wait()
    come[4].wait()

    def restore():
        l[...] = l_prev[...]
        again = pltpu.make_async_copy(o_hbm, o, sems_in.at[4])
        again.start()
        again.wait()

    col = factors.at[0]
    attend(covered, q, k, vt, e, o, l, m, mb, col, True, starts, count, lambda pair: None, restore)
    for copy in late[:2]:
        copy.start()

    invt = 1.0 / l[...]
    factors[0] = turned_rows(invt * jnp.exp2(mb[...] - m[...]))
    factors[1] = turned_rows(invt * jnp.exp2(m_prev[...] - m[...]))

    def waits(*which):
        def wait():
            for n in which:
                come[n].wait()

        return wait

    def fetch_late():
        for copy in late[2:7]:
            copy.start()

    middle(
        count,
        o,
        invt,
        x,
        cot,
        go,
        got,
        g_one,
        lesst,
        hat_ref,
        low_ref,
        pool,
        scale_ref,
        bias_ref,
        bias_up_ref,
        gain_ref,
        w_out,
        w_up,
        w_down,
        (waits(5, 6), waits(7), waits(8), waits(9, 10)),
        (leave[0].start, fetch_late),
    )
    less[...] = lesst[...].T.astype(bf16)
    o[...] = jnp.zeros_like(o)

    def one_chip(chip):
        own = chip == 1

        @pl.when(own)
        def _():
            late[0].wait()
            late[1].wait()

        def ready(pair):
            @pl.when(own)
            def _():
                copy_e(pair).wait()

        def done(pair):
            @pl.when(jnp.logical_not(own))
            def _():
                copy_e(pair).start()

        attend_back(
            go,
            got,
            qt,
            less,
            factors.at[chip],
            kv.at[pl.ds(2 * chip, 2)],
            turned.at[chip],
            e,
            o,
            [gvt_all.at[:, span_of(2 - 2 * chip + block, rows)] for block in range(2)],
            (gkv.at[0], gkv.at[1]),
            scores,
            ready,
            done,
        )

        @pl.when(own)
        def _():
            leave[1].wait()
            leave[2].wait()

        out = product_back(both(gkv), wkv[...])
        for block in range(2):
            for at in row_chunks(rows):
                part = out[block * rows + at.start : block * rows + at.stop]
                x_far[block, at, :] = part.astype(bf16)

        @pl.when(own)
        def _():
            leave[4].start()

        @pl.when(jnp.logical_not(own))
        def _():
            leave[1].start()
            leave[2].start()
            late[7].start()

    for_each(2, one_chip)
    for at in row_chunks(width):
        got[at, :] = (o[at, :] * HEAD ** (-0.5)).astype(bf16)
    go[...] = got[...].T
    leave[5].start()
    for at in row_chunks(rows):
        g_one[at, :] += x_far[0, at, :].astype(f32)
    leave[3].start()
    for copy in late[2:]:
        copy.wait()
    bt = kt
    rank = a.shape[1]
    total_ref[...] = jnp.zeros_like(total_ref)
    eye = lax.broadcasted_iota(jnp.int32, (PAIR, PAIR), 0) == lanes((PAIR, PAIR))
    for n in range(2):
        if n == 0:
            outer = product(got[...], x_all[0:rows, :])
        else:
            outer = product(gvt_all[...], x_all[...])
        mixed = product(outer.astype(bf16), a[...])
        for_d = jnp.zeros((1, rank), f32)
        for at in row_chunks(width, PAIR):
            part = mixed[at] * bt[at, :].astype(f32)
            column = jnp.sum(jnp.where(eye, b_ref[n : n + 1, at], 0.0), axis=1, keepdims=True)
            for_d = for_d + jnp.sum(part * column, axis=0, keepdims=True)
            sums = jnp.sum(part * d_ref[n : n + 1, :], axis=1, keepdims=True)
            total_ref[2 + n : 3 + n, at] = jnp.sum(jnp.where(eye, sums, 0.0), axis=0, keepdims=True)
        total_ref[n : n + 1, :] = for_d
    for copy in (leave[0], *leave[3:]):
        copy.wait()


def far(small, large):
    w_all, x_two, x_three, q, o, w_out, w_up, w_down = large[:8]
    a = large[-2]
    rows, width = x_two.shape
    hidden = w_up.shape[1]
    rank = a.shape[1]
    low, square, expo = (rows, width), (width, width), (HEADS, rows, 2 * rows)
    turned, row, stat = (width, 2 * rows), (ROWS, rows), (rows, PAIR)
    flat = (width, rows)
    places = [HBM, ANY, ANY] + [HBM] * (len(large) - 3)
    places[11] = ANY
    return call(
        far_kernel,
        "far",
        (*small, *large),
        [SMEM] * 2 + [VMEM] * (len(small) - 2) + places,
        [
            (VMEM, (4, rank), f32),
            (HBM, low, bf16),
            (HBM, low, f32),
            (HBM, low, bf16),
            (HBM, low, bf16),
            (HBM, low, bf16),
            (HBM, low, bf16),
        ],
        buffers((width, 2 * width), (2,) + low, low)
        + buffers(flat, dtype=f32)
        + buffers(square, (width, hidden), (hidden, width), low, low, flat)
        + buffers(low, dtype=f32)
        + buffers(flat, (4,) + low, (2,) + turned, expo)
        + buffers((2 * hidden // (2 * rows), rows, 2 * rows))
        + buffers((2, rows, 2 * width), (2, rows, 2 * rows))
        + buffers(row, row, row, (PAIR, rows), dtype=f32)
        + buffers(stat)
        + buffers((2,) + stat, stat, dtype=f32)
        + buffers(low)
        + [
            pltpu.SemaphoreType.DMA((11,)),
            pltpu.SemaphoreType.DMA((width // PAIR,)),
            pltpu.SemaphoreType.DMA((8,)),
            pltpu.SemaphoreType.DMA((6,)),
        ],
        160 * rows * rows * width + 30 * rows * width * width + 8 * rows * width * hidden,
        60 * 1024 * 1024,
        2 * HEADS * rows * rows + 2 * rows * hidden,
    )


def tree_sum(terms):
    while len(terms) > 1:
        terms = [terms[n] + terms[n + 1] for n in range(0, len(terms), 2)]
    return terms[0]


def step_kernel(count, *refs):
    totals = tree_sum([ref[...] for ref in refs[:count]])
    weights = refs[count : count + 6]
    outs = refs[count + 6 :]
    for n in range(2):
        weight, moment, second = weights[3 * n : 3 * n + 3]
        grad = totals[2 * n : 2 * n + 2, : weight.shape[1]]
        moment_new, second_new, weight_new = adamw(weight[...], moment[...], second[...], grad)
        outs[2 * n][...] = moment_new
        outs[2 * n + 1][...] = second_new
        outs[4 + n][...] = weight_new
        outs[6 + n][...] = weight_new.astype(bf16)


def step(terms, weights):
    d, b = weights[0].shape, weights[3].shape
    shapes = [(s, f32) for s in (d, d, b, b, d, b)] + [(d, bf16), (b, bf16)]
    return pl.pallas_call(
        partial(step_kernel, len(terms)),
        in_specs=[VMEM] * (len(terms) + 6),
        out_specs=[VMEM] * 8,
        out_shape=[shaped(*one) for one in shapes],
        name="step",
    )(*terms, *weights)


def swap(value, axis, size, mask):
    return lax.ppermute(value, axis, [(i, i ^ mask) for i in range(size)])


def partners(value, axis, size, stride):
    radix = min(4, size // stride)
    return [value] + [swap(value, axis, size, n * stride) for n in range(1, radix)]


def per_device(
    seq_size,
    dp_size,
    tokens,
    lengths,
    cotangent,
    w_query,
    w_key,
    w_value,
    w_out,
    w_up,
    w_down,
    shared_a,
    shared_b,
    vec_biases,
    bias_up,
    norm_gains,
    scale_d,
    scale_b,
    mom_d,
    sec_d,
    mom_b,
    sec_b,
):
    _, local_len, width = tokens.shape
    x = tokens.reshape(local_len, width)
    x_one = swap(x, "seq", seq_size, 1)
    x_two = swap(x, "seq", seq_size, 2)
    fast, l, m, e_near, o, q, qt, v_near, kt_near, w_all, b_turned = near(
        lengths, scale_d, scale_b, vec_biases, x, w_key, shared_a, shared_b, w_query, w_value, x_one
    )
    x_two, o = lax.optimization_barrier((x_two, o))
    x_three = swap(x_two, "seq", seq_size, 1)
    totals, activations, g_one, two, three, one, gq = far(
        (
            lengths,
            fast,
            vec_biases,
            bias_up.reshape(1, -1),
            norm_gains,
            scale_d,
            scale_b,
            l,
            m,
        ),
        (
            w_all,
            x_two,
            x_three,
            q,
            o,
            w_out,
            w_up,
            w_down,
            x,
            cotangent.reshape(local_len, width),
            qt,
            x_one,
            v_near,
            kt_near,
            e_near,
            shared_a,
            b_turned,
        ),
    )
    from_three = swap(three, "seq", seq_size, 1)
    joined = (two.astype(f32) + from_three.astype(f32)).astype(bf16)
    terms = partners(totals, "seq", seq_size, 1)
    joined, *terms = lax.optimization_barrier((joined, *terms))
    from_two = swap(joined, "seq", seq_size, 2)
    from_one = swap(one, "seq", seq_size, 1)
    stride = 1
    while stride < dp_size:
        terms = partners(tree_sum(terms), "dp", dp_size, stride)
        stride *= len(terms)
    moment_d, second_d, moment_b, second_b, new_d, new_b, copy_d, copy_b = step(
        terms, (scale_d, mom_d, sec_d, scale_b, mom_b, sec_b)
    )
    rest = lax.optimization_barrier(g_one + product_back(gq, w_all[:, :width]))
    grad_inputs = rest + from_one.astype(f32) + from_two.astype(f32)
    return (
        activations.reshape(tokens.shape),
        grad_inputs.reshape(tokens.shape),
        moment_d,
        second_d,
        moment_b,
        second_b,
        new_d,
        new_b,
        copy_d,
        copy_b,
    )


def solution(mesh):
    rows = P("dp", "seq", None)
    return jax.shard_map(
        partial(per_device, mesh.shape["seq"], mesh.shape["dp"]),
        mesh=mesh,
        in_specs=(rows, P("dp"), rows) + (P(),) * 17,
        out_specs=(rows, rows) + (P(),) * 8,
        check_vma=False,
    )
```
